256 devices in a mesh: outer: 16 (over y, x), inner: 16 (over z, core).
Axes of the slice: x: 4, y: 4, z: 8, core: 2. Of those that a mesh axis runs over, the one named last changes fastest.
Arguments:
- tokens: bfloat16 [98304, 1024], P(('outer', 'inner')), may hold values from -6 to 6
- log_decay: float32 [98304, 16], P(('outer', 'inner')), may hold values from -1 to 0, as said below
- query_weight: bfloat16 [1024, 1024], replicated, may hold values from -0.1875 to 0.1875
- key_weight: bfloat16 [1024, 1024], replicated, may hold values from -0.1875 to 0.1875
- value_weight: bfloat16 [1024, 1024], replicated, may hold values from -0.1875 to 0.1875
- norm_gain: float32 [1024], replicated, may hold values from 0.1 to 1.9
- output_weight: bfloat16 [1024, 1024], replicated, may hold values from -0.1875 to 0.1875
Outputs:
- mixed: bfloat16 [98304, 1024], P(('outer', 'inner'))
The draws below stay inside these ranges and needn't reach their ends.
Inputs may be any that keep to these rules, and one draw needn't show every extreme that they name: log_decay is negative.
All inputs are finite; a program needn't handle non-finite values.
Results may differ from the reference program's by a relative error of at most 0.0063.
Values sent between devices are 32-bit elements; how exact they have to be, the bound alone decides.
A program may use at most 320 MiB of HBM per device.

```python
import math
import jax
import jax.numpy as jnp
from jax import lax

D = 1024
HEAD_COUNT = 16
HEAD_DIM = 64
TOK_DEV = 384
TOKEN_COUNT = 98304


def draw_log_decay(key, part):
    token_parts = jax.random.split(key, 6)
    slow_share = 0.5
    picked = jax.random.uniform(token_parts[0], (HEAD_COUNT,)) < slow_share
    fast_rate = jnp.exp(jax.random.uniform(token_parts[1], (HEAD_COUNT,), minval=math.log(1.0 / 1000.0), maxval=math.log(1.0 / 40.0)))
    slow_rate = 0.25 * math.log(10.0) / TOKEN_COUNT
    base = jnp.where(picked, slow_rate, fast_rate)
    block_count = TOKEN_COUNT // TOK_DEV
    block_factor = jnp.exp(jax.random.uniform(token_parts[2], (block_count,), minval=-math.log(2.0), maxval=math.log(2.0)))
    positions = jnp.arange(TOKEN_COUNT) // TOK_DEV
    rough = jnp.exp(jax.random.uniform(token_parts[3], (TOKEN_COUNT, HEAD_COUNT), minval=-math.log(2.0), maxval=math.log(2.0)))
    decay_rate = base[None, :] * block_factor[positions][:, None] * rough
    decay_power = jax.random.uniform(token_parts[4], (TOKEN_COUNT, HEAD_COUNT)) < 2.0 / TOKEN_COUNT
    training_loss = jnp.log(jax.random.uniform(token_parts[5], (TOKEN_COUNT, HEAD_COUNT), minval=0.5, maxval=0.8))
    return (jnp.where(decay_power, training_loss, 0.0) - decay_rate).astype(jnp.float32)


def steps_of(stream_key, shape, pieces, least, top_value):
    def one(dim, shards_of):
        draws = jax.random.uniform(jax.random.fold_in(jax.random.fold_in(stream_key, 6), dim), (shards_of,), jnp.float32, least / len(pieces), top_value / len(pieces))
        return jnp.repeat(jnp.exp(draws), shape[dim] // shards_of).reshape((-1,) + (1,) * (len(shape) - dim - 1))

    factor_of = one(*pieces[0])
    for cut in pieces[1:]:
        factor_of = factor_of * one(*cut)
    return factor_of


def bell_draw(key, shape, spread, bound, cuts=(), dtype=jnp.bfloat16):
    values = jax.random.normal(key, shape, jnp.float32) * spread
    if len(cuts) > 0:
        values = steps_of(key, shape, cuts, -0.22, 0.18) * values
    return jnp.clip(values, min=-bound, max=bound).astype(dtype)


def setup_inputs(seed: int = 0) -> dict:
    seeds = jax.random.split(jax.random.key(seed), 8)
    tokens = bell_draw(seeds[0], (TOKEN_COUNT, D), 1.0, 6.0, ((0, 256),))
    log_decay = draw_log_decay(jax.random.fold_in(seeds[7], 71), 0)
    query_weight = bell_draw(seeds[2], (D, D), D ** -0.5, 0.1875)
    key_weight = bell_draw(seeds[3], (D, D), D ** -0.5, 0.1875)
    value_weight = bell_draw(seeds[4], (D, D), D ** -0.5, 0.1875)
    norm_gain = jnp.clip(1.0 + 0.18 * jax.random.normal(seeds[5], (D,), jnp.float32), 0.1, 1.9)
    output_weight = bell_draw(seeds[6], (D, D), D ** -0.5, 0.1875)
    return {"tokens": tokens, "log_decay": log_decay, "query_weight": query_weight, "key_weight": key_weight, "value_weight": value_weight, "norm_gain": norm_gain, "output_weight": output_weight}


def local_head(q_head, k_head, v_head, g_head):
    cum = jnp.cumsum(g_head)
    count = cum.shape[0]
    rows = lax.broadcasted_iota(jnp.int32, (count, count), 0)
    cols = lax.broadcasted_iota(jnp.int32, (count, count), 1)
    lower = cols <= rows
    diff = jnp.where(lower, cum[:, None] - cum[None, :], 0.0)
    decay = jnp.where(lower, jnp.exp(diff), 0.0)
    scores = jnp.dot(q_head, k_head.T, preferred_element_type=jnp.float32)
    weights = (scores * decay).astype(jnp.bfloat16)
    intra = jnp.dot(weights, v_head, preferred_element_type=jnp.float32)
    last = cum[-1]
    scaled = (k_head.astype(jnp.float32) * jnp.exp(last - cum)[:, None]).astype(jnp.bfloat16)
    local = jnp.dot(scaled.T, v_head, preferred_element_type=jnp.float32)
    return (intra, local, jnp.exp(last))

def project(block, query_weight, key_weight, value_weight, heads):
    count = block.shape[0]
    queries = jax.nn.silu(jnp.dot(block, query_weight, preferred_element_type=jnp.float32)).astype(jnp.bfloat16)
    keys = jax.nn.silu(jnp.dot(block, key_weight, preferred_element_type=jnp.float32)).astype(jnp.bfloat16)
    value_rows = jnp.dot(block, value_weight, preferred_element_type=jnp.float32).astype(jnp.bfloat16)
    split = lambda arr: arr.reshape(count, heads, -1).transpose(1, 0, 2)
    return (split(queries), split(keys), split(value_rows))

def finish(intra, queries, g_block, incoming, norm_gain, output_weight):
    cum = jnp.cumsum(g_block, axis=0)
    qfloat = queries.astype(jnp.float32)
    inter = jnp.einsum('htd,hde->the', qfloat, incoming, precision=lax.Precision.HIGHEST) * jnp.exp(cum)[:, :, None]
    attended = intra.transpose(1, 0, 2) + inter
    scale = lax.rsqrt(lax.optimization_barrier(jnp.mean(attended * attended, axis=-1, keepdims=True)) + 1e-05)
    count = attended.shape[0]
    normalized_output = ((attended * scale).reshape(count, -1) * norm_gain).astype(jnp.bfloat16)
    return jnp.dot(normalized_output, output_weight, preferred_element_type=jnp.float32).astype(jnp.bfloat16)

def reference(tokens, log_decay, query_weight, key_weight, value_weight, norm_gain, output_weight):
    blocks = TOKEN_COUNT // TOK_DEV
    token_blocks = tokens.reshape(blocks, TOK_DEV, D)
    decay_blocks = log_decay.reshape(blocks, TOK_DEV, HEAD_COUNT)

    def step(state, item):
        block, g_block = item
        queries, keys, value_rows = project(block, query_weight, key_weight, value_weight, HEAD_COUNT)
        intra, local, fall = lax.map(lambda token_parts: local_head(*token_parts), (queries, keys, value_rows, g_block.T))
        result = finish(intra, queries, g_block, state, norm_gain, output_weight)
        return (fall[:, None, None] * state + local, result)
    start = jnp.zeros((HEAD_COUNT, HEAD_DIM, HEAD_DIM), jnp.float32)
    final, outputs = lax.scan(step, start, (token_blocks, decay_blocks))
    return outputs.reshape(TOKEN_COUNT, D)
```

```python
import functools

import jax
import jax.numpy as jnp
from jax import lax
from jax.experimental import pallas as pl
from jax.experimental.pallas import tpu as pltpu
from jax.sharding import PartitionSpec as P

F32 = jnp.float32
BF16 = jnp.bfloat16
HEADS = 16
HEAD = 64
PAIRS = 8
PAIR = 128
QUADS = 4
QUAD = 256
TOKENS = 384
SUB = 128
WIDTH = 1024
HALF = 32


def dot(a, b):
    return jnp.dot(a, b, preferred_element_type=F32)


def dot_nt(a, b):
    return lax.dot_general(a, b, (((1,), (1,)), ((), ())), preferred_element_type=F32)


def dot_tn(a, b):
    return lax.dot_general(a, b, (((0,), (0,)), ((), ())), preferred_element_type=F32)


def silu(x):
    return x * (0.5 * jnp.tanh(0.5 * x) + 0.5)


def split3(x):
    hi = x.astype(BF16)
    rest = x - hi.astype(F32)
    mid = rest.astype(BF16)
    return hi, mid, (rest - mid.astype(F32)).astype(BF16)


def kernel(
    outers,
    chips,
    tok_hbm,
    decay_hbm,
    wq_hbm,
    wk_hbm,
    wv_hbm,
    gain_hbm,
    wo_hbm,
    out_hbm,
    tok,
    decay,
    wq,
    wk,
    wv,
    gain,
    wo,
    q,
    k,
    v,
    cum_b,
    cum_t,
    intra,
    local,
    crossed,
    chip,
    in1,
    prefix,
    total,
    in2,
    out3,
    in3,
    give,
    state,
    f_own,
    f_sib,
    f_chip,
    f_in1,
    f_group,
    f_in2,
    normed,
    out,
    load_sem,
    store_sem,
    f0_sem,
    f1_sem,
    f2_sem,
    s0_sem,
    s1_sem,
    s2_sem,
    s3_sem,
    s4_sem,
):
    o = lax.axis_index("outer")
    inner = lax.axis_index("inner")
    z, c = inner // 2, inner % 2
    sibling = (o, z * 2 + 1 - c)

    def along(d):
        return (z + d) % chips

    def at_z(other):
        return (o, other * 2 + c)

    def at_o(other):
        return (other, inner)

    def load(src, dst, n):
        copy = pltpu.make_async_copy(src, dst, load_sem.at[n])
        copy.start()
        return copy

    load_decay = load(decay_hbm, decay, 0)
    load_tok = load(tok_hbm, tok, 1)
    load_k, load_v, load_q, load_o = [], [], [], []
    for n in range(QUADS):
        cols = pl.ds(n * QUAD, QUAD)
        load_k.append(load(wk_hbm.at[:, cols], wk.at[n], 2 + n))
        load_v.append(load(wv_hbm.at[:, cols], wv.at[n], 6 + n))
    for n in range(QUADS):
        cols = pl.ds(n * QUAD, QUAD)
        load_q.append(load(wq_hbm.at[:, cols], wq.at[n], 10 + n))
    for n in range(QUADS):
        cols = pl.ds(n * QUAD, QUAD)
        load_o.append(load(wo_hbm.at[:, cols], wo.at[n], 14 + n))
    load_gain = load(gain_hbm, gain, 18)

    barrier = pltpu.get_barrier_semaphore()
    pl.semaphore_signal(barrier, inc=1, device_id=sibling, device_id_type=MESH)
    for d in range(1, chips):
        pl.semaphore_signal(barrier, inc=1, device_id=at_z(along(d)), device_id_type=MESH)
    for d in range(1, outers):
        pl.semaphore_signal(barrier, inc=1, device_id=at_o((o + d) % outers), device_id_type=MESH)

    sent = []

    def send(src, dst, sems, slot_out, slot_in, device):
        copy = pltpu.make_async_remote_copy(
            src_ref=src,
            dst_ref=dst,
            send_sem=sems.at[0, slot_out],
            recv_sem=sems.at[1, slot_in],
            device_id=device,
            device_id_type=MESH,
        )
        copy.start()
        return copy

    def arrived(dst, sems, slot_in):
        pltpu.make_async_remote_copy(
            src_ref=dst,
            dst_ref=dst,
            send_sem=sems.at[0, slot_in],
            recv_sem=sems.at[1, slot_in],
            device_id=sibling,
            device_id_type=MESH,
        ).wait_recv()

    lane = lax.broadcasted_iota(jnp.int32, (1, PAIR), 1)
    first = lane < HEAD
    rows = lax.broadcasted_iota(jnp.int32, (TOKENS, TOKENS), 0)
    cols = lax.broadcasted_iota(jnp.int32, (TOKENS, TOKENS), 1)
    triangle = jnp.where(cols <= rows, 1.0, 0.0).astype(BF16)
    load_decay.wait()
    hi, mid, lo = split3(decay[...])
    cum = dot(triangle, hi) + (dot(triangle, mid) + dot(triangle, lo))
    for h in range(HEADS):
        cum_b[h] = jnp.broadcast_to(cum[:, h : h + 1], (TOKENS, PAIR))
    wide = jnp.concatenate([cum, jnp.zeros((TOKENS, PAIR - HEADS), F32)], axis=1)
    turned = wide.T
    for h in range(HEADS):
        cum_t[h] = turned[h : h + 1, :]

    def pair_cum(p):
        return jnp.where(first, cum_b[2 * p], cum_b[2 * p + 1])

    for p in range(PAIRS):
        last = jnp.where(
            first, cum_b[2 * p, TOKENS - 1 : TOKENS, :], cum_b[2 * p + 1, TOKENS - 1 : TOKENS, :]
        )
        f_own[p : p + 1, :] = jnp.exp(last)

    pl.semaphore_wait(barrier, chips + outers - 1)
    sent.append(send(f_own, f_sib, f0_sem, 0, 0, sibling))

    load_tok.wait()
    for n in range(QUADS):
        load_k[n].wait()
        keys = silu(dot(tok[...], wk[n])).astype(BF16)
        load_v[n].wait()
        values = dot(tok[...], wv[n]).astype(BF16)
        for e in range(2):
            p = 2 * n + e
            part = slice(e * PAIR, (e + 1) * PAIR)
            k[p] = keys[:, part]
            v[p] = values[:, part]
            run = pair_cum(p)
            left = jnp.exp(run[TOKENS - 1 :, :] - run)
            scaled = (keys[:, part].astype(F32) * left).astype(BF16)
            outer = dot_tn(scaled, values[:, part])
            own = jnp.where(first, outer[:HEAD], outer[HEAD:])
            local[p] = own.reshape(2, HALF, PAIR)
        two = pl.ds(2 * n, 2)
        sent.append(send(local.at[two, 1 - c], crossed.at[two], s0_sem, n, n, sibling))

    arrived(f_sib, f0_sem, 0)
    fall0 = jnp.where(c == 0, f_own[...], f_sib[...])
    fall1 = jnp.where(c == 0, f_sib[...], f_own[...])
    f_chip[...] = fall0 * fall1
    f_in1[z] = fall0 * fall1
    for d in range(1, chips):
        sent.append(send(f_chip, f_in1.at[z], f1_sem, d, z, at_z(along(d))))

    def project_queries(n):
        load_q[n].wait()
        queries = silu(dot(tok[...], wq[n])).astype(BF16)
        q[2 * n] = queries[:, :PAIR]
        q[2 * n + 1] = queries[:, PAIR:]

    def attend(p):
        def head(e):
            keep = first if e == 0 else jnp.logical_not(first)
            h = 2 * p + e
            pieces = []
            for i in range(TOKENS // SUB):
                here = pl.ds(i * SUB, SUB)
                upto = (i + 1) * SUB
                mine = jnp.where(keep, q[p, here, :].astype(F32), 0.0).astype(BF16)
                scores = dot_nt(mine, k[p, :upto, :])
                row = cum_b[h, here, :]
                blocks = []
                for j in range(i + 1):
                    diff = row - cum_t[h, :, j * SUB : (j + 1) * SUB]
                    if j == i:
                        r = lax.broadcasted_iota(jnp.int32, (SUB, SUB), 0)
                        s = lax.broadcasted_iota(jnp.int32, (SUB, SUB), 1)
                        diff = jnp.where(s <= r, diff, -jnp.inf)
                    blocks.append(
                        (scores[:, j * SUB : (j + 1) * SUB] * jnp.exp(diff)).astype(BF16)
                    )
                weights = jnp.concatenate(blocks, axis=1)
                pieces.append(dot(weights, v[p, :upto, :]))
            return pieces

        for i, (one, two) in enumerate(zip(head(0), head(1))):
            intra[p, i * SUB : (i + 1) * SUB, :] = jnp.where(first, one, two)

    def attend_pairs(start, stop):
        def body(p, carry):
            attend(p)
            return carry

        lax.fori_loop(start, stop, body, 0)

    for n in range(QUADS):
        project_queries(n)

    for n in range(QUADS):
        arrived(crossed.at[pl.ds(2 * n, 2)], s0_sem, n)
    for p in range(PAIRS):
        mine = local[p, c]
        theirs = crossed[p]
        f1 = fall1[p : p + 1, :]
        chip[p] = jnp.where(c == 0, f1 * mine + theirs, f1 * theirs + mine)
    in1[z] = chip[z]
    for d in range(1, chips):
        t = along(d)
        sent.append(send(chip.at[t], in1.at[z], s1_sem, d, z, at_z(t)))

    for d in range(1, chips):
        arrived(f_in1.at[along(d)], f1_sem, along(d))
    group = f_in1[0]
    for i in range(1, chips):
        group = group * f_in1[i]
    f_group[...] = group
    later = []
    for d in range(1, outers):

        def go(d=d):
            send(f_group, f_in2.at[o], f2_sem, d, o, at_o(o + d))

        pl.when(o + d < outers)(go)

    attend_pairs(0, 2)

    for d in range(1, chips):
        arrived(in1.at[along(d)], s1_sem, along(d))
    run = jnp.zeros((HALF, PAIR), F32)
    for i in range(chips):
        prefix[i] = run
        run = f_in1[i, pl.ds(z, 1), :] * run + in1[i]
    total[...] = run
    for d in range(1, outers):

        def go(d=d):
            send(total, in2.at[o], s2_sem, d, o, at_o(o + d))

        pl.when(o + d < outers)(go)

    attend_pairs(2, 4)

    def earlier(i, before):
        arrived(f_in2.at[i], f2_sem, i)
        arrived(in2.at[i], s2_sem, i)
        return f_in2[i, pl.ds(z, 1), :] * before + in2[i]

    before = lax.fori_loop(0, o, earlier, jnp.zeros((HALF, PAIR), F32))
    fall = jnp.ones((1, PAIR), F32)
    for i in range(chips):
        out3[i] = fall * before + prefix[i]
        fall = fall * f_in1[i, pl.ds(z, 1), :]
    in3[z] = out3[z]
    for d in range(1, chips):
        t = along(d)
        sent.append(send(out3.at[t], in3.at[z], s3_sem, d, z, at_z(t)))

    attend_pairs(4, 8)

    for d in range(0, chips):
        p = along(d)
        if d > 0:
            arrived(in3.at[p], s3_sem, p)
        enters = in3[p]
        first_local = jnp.where(c == 0, local[p, 0], crossed[p])
        f0 = jnp.where(c == 0, f_own[pl.ds(p, 1), :], f_sib[pl.ds(p, 1), :])
        middle = f0 * enters + first_local
        state[p, c] = jnp.where(c == 0, enters, middle)
        give[p] = jnp.where(c == 0, middle, enters)
        sent.append(send(give.at[p], state.at[p, c], s4_sem, p, p, sibling))

    load_gain.wait()
    r = lax.broadcasted_iota(jnp.int32, (PAIR, PAIR), 0) // HEAD
    s = lax.broadcasted_iota(jnp.int32, (PAIR, PAIR), 1) // HEAD
    means = jnp.where(r == s, 1.0 / HEAD, 0.0).astype(BF16)
    for p in range(PAIRS):
        arrived(state.at[p, 1 - c], s4_sem, p)
        flat = state[p].reshape(HEAD, PAIR)
        both = jnp.concatenate([jnp.where(first, flat, 0.0), jnp.where(first, 0.0, flat)], axis=0)
        hi = both.astype(BF16)
        lo = (both - hi.astype(F32)).astype(BF16)
        inter = dot(q[p], hi) + dot(q[p], lo)
        attended = intra[p] + jnp.exp(pair_cum(p)) * inter
        mean = dot((attended * attended).astype(BF16), means)
        part = slice(p * PAIR, (p + 1) * PAIR)
        normed[:, part] = (attended * lax.rsqrt(mean + 1e-5) * gain[:, part]).astype(BF16)

    stores = []
    for n in range(QUADS):
        load_o[n].wait()
        out[n] = dot(normed[...], wo[n]).astype(BF16)
        copy = pltpu.make_async_copy(
            out.at[n], out_hbm.at[:, pl.ds(n * QUAD, QUAD)], store_sem.at[n]
        )
        copy.start()
        stores.append(copy)

    for copy in sent:
        copy.wait_send()
    for d in range(1, outers):

        def finish(d=d):
            for src, sems in ((f_group, f2_sem), (total, s2_sem)):
                pltpu.make_async_remote_copy(
                    src_ref=src,
                    dst_ref=src,
                    send_sem=sems.at[0, d],
                    recv_sem=sems.at[1, d],
                    device_id=sibling,
                    device_id_type=MESH,
                ).wait_send()

        pl.when(o + d < outers)(finish)
    for copy in stores:
        copy.wait()


MESH = pl.DeviceIdType.MESH


def solution(mesh):
    outers, chips = mesh.shape["outer"], mesh.shape["inner"] // 2

    def shards(tokens, log_decay, query_weight, key_weight, value_weight, norm_gain, output_weight):
        vmem = pltpu.VMEM
        dma = pltpu.SemaphoreType.DMA
        weight = vmem((QUADS, WIDTH, QUAD), BF16)
        by_pair = vmem((PAIRS, TOKENS, PAIR), BF16)
        unit = (HALF, PAIR)
        tile = (PAIRS, PAIR)
        return pl.pallas_call(
            functools.partial(kernel, outers, chips),
            out_shape=jax.ShapeDtypeStruct((TOKENS, WIDTH), BF16),
            in_specs=[pl.BlockSpec(memory_space=pl.ANY)] * 7,
            out_specs=pl.BlockSpec(memory_space=pl.ANY),
            scratch_shapes=[
                vmem((TOKENS, WIDTH), BF16),
                vmem((TOKENS, HEADS), F32),
                weight,
                weight,
                weight,
                vmem((1, WIDTH), F32),
                weight,
                by_pair,
                by_pair,
                by_pair,
                vmem((HEADS, TOKENS, PAIR), F32),
                vmem((HEADS, 1, TOKENS), F32),
                vmem((PAIRS, TOKENS, PAIR), F32),
                vmem((PAIRS, 2) + unit, F32),
                vmem((PAIRS,) + unit, F32),
                vmem((PAIRS,) + unit, F32),
                vmem((chips,) + unit, F32),
                vmem((chips,) + unit, F32),
                vmem(unit, F32),
                vmem((outers,) + unit, F32),
                vmem((chips,) + unit, F32),
                vmem((PAIRS,) + unit, F32),
                vmem((PAIRS,) + unit, F32),
                vmem((PAIRS, 2) + unit, F32),
                vmem(tile, F32),
                vmem(tile, F32),
                vmem(tile, F32),
                vmem((chips,) + tile, F32),
                vmem(tile, F32),
                vmem((outers,) + tile, F32),
                vmem((TOKENS, WIDTH), BF16),
                vmem((QUADS, TOKENS, QUAD), BF16),
                dma((19,)),
                dma((QUADS,)),
                dma((2, 1)),
                dma((2, chips)),
                dma((2, outers)),
                dma((2, QUADS)),
                dma((2, chips)),
                dma((2, outers)),
                dma((2, chips)),
                dma((2, PAIRS)),
            ],
            compiler_params=pltpu.CompilerParams(
                collective_id=0, has_side_effects=True, vmem_limit_bytes=48 << 20
            ),
            cost_estimate=pl.CostEstimate(
                flops=4 * 10**9, bytes_accessed=10 << 20, transcendentals=2 * 10**6
            ),
        )(
            tokens,
            log_decay,
            query_weight,
            key_weight,
            value_weight,
            norm_gain.reshape(1, WIDTH),
            output_weight,
        )

    in_specs = (P(("outer", "inner"), None), P(("outer", "inner"), None), P(), P(), P(), P(), P())
    out_specs = P(("outer", "inner"), None)
    return jax.shard_map(shards, mesh=mesh, in_specs=in_specs, out_specs=out_specs, check_vma=False)
```

```python
import functools

import jax
import jax.numpy as jnp
from jax import lax
from jax.experimental import pallas as pl
from jax.experimental.pallas import tpu as pltpu
from jax.sharding import PartitionSpec as P

F32 = jnp.float32
BF16 = jnp.bfloat16
HEADS = 16
HEAD = 64
PAIRS = 8
PAIR = 128
QUADS = 4
QUAD = 256
TOKENS = 384
SUB = 128
WIDTH = 1024
SIDE = 4
HALF = 32


def dot(a, b):
    return jnp.dot(a, b, preferred_element_type=F32)


def dot_nt(a, b):
    return lax.dot_general(a, b, (((1,), (1,)), ((), ())), preferred_element_type=F32)


def dot_tn(a, b):
    return lax.dot_general(a, b, (((0,), (0,)), ((), ())), preferred_element_type=F32)


def silu(x):
    return x * (0.5 * jnp.tanh(0.5 * x) + 0.5)


def split3(x):
    hi = x.astype(BF16).astype(F32)
    rest = x - hi
    mid = rest.astype(BF16).astype(F32)
    return jnp.concatenate([hi, mid, rest - mid], axis=0)


def kernel(
    outers,
    chips,
    tok_hbm,
    decay_hbm,
    wq_hbm,
    wk_hbm,
    wv_hbm,
    gain_hbm,
    wo_hbm,
    out_hbm,
    tok,
    decay,
    wq,
    wk,
    wv,
    gain,
    wo,
    q,
    k,
    v,
    cum_b,
    cum_t,
    intra,
    local,
    crossed,
    chip,
    in1,
    prefix,
    total,
    in2,
    out3,
    in3,
    give,
    state,
    f_own,
    f_sib,
    f_chip,
    f_in1,
    normed,
    partial,
    out,
    load_sem,
    store_sem,
    f0_sem,
    f1_sem,
    s0_sem,
    s1_sem,
    s2_sem,
    s3_sem,
    s4_sem,
):
    o = lax.axis_index("outer")
    inner = lax.axis_index("inner")
    z, c = inner // 2, inner % 2
    y, x = o // SIDE, o % SIDE
    sibling = (o, z * 2 + 1 - c)

    def along(d):
        return (z + d) % chips

    def at_z(other):
        return (o, other * 2 + c)

    far_z = sorted(range(1, chips), key=lambda d: -min(d, chips - d))
    near_z = [0] + far_z[::-1]
    plane = sorted(
        ((a, b) for a in range(outers // SIDE) for b in range(SIDE) if (a, b) != (0, 0)),
        key=lambda t: -(min(t[0], outers // SIDE - t[0]) + min(t[1], SIDE - t[1])),
    )

    def group_at(a, b):
        return (y + a) % (outers // SIDE) * SIDE + (x + b) % SIDE

    def load(src, dst, n):
        copy = pltpu.make_async_copy(src, dst, load_sem.at[n])
        copy.start()
        return copy

    mine = z // 2
    odd = z % 2
    order = [(mine + 2) % QUADS, (mine + 1 + 2 * odd) % QUADS, (mine + 3 - 2 * odd) % QUADS, mine]

    load_decay = load(decay_hbm, decay, 0)
    load_tok = load(tok_hbm, tok, 1)
    load_k, load_v, load_q, load_o = [], [], [], []
    for n in range(QUADS):
        cols = pl.ds(pl.multiple_of(order[n] * QUAD, QUAD), QUAD)
        load_k.append(load(wk_hbm.at[:, cols], wk.at[n], 2 + n))
        load_v.append(load(wv_hbm.at[:, cols], wv.at[n], 6 + n))
    for n in range(QUADS):
        load_q.append(load(wq_hbm.at[:, pl.ds(n * QUAD, QUAD)], wq.at[n], 10 + n))
    for n in range(PAIRS):
        load_o.append(load(wo_hbm.at[pl.ds(n * PAIR, PAIR)], wo.at[n], 14 + n))
    load_gain = load(gain_hbm, gain, 22)

    barrier = pltpu.get_barrier_semaphore()
    pl.semaphore_signal(barrier, inc=1, device_id=sibling, device_id_type=MESH)
    for d in range(1, chips):
        pl.semaphore_signal(barrier, inc=1, device_id=at_z(along(d)), device_id_type=MESH)
    for a, b in plane:
        pl.semaphore_signal(
            barrier, inc=1, device_id=(group_at(a, b), inner), device_id_type=MESH
        )

    sent = []

    def remote(src, dst, sems, slot_out, slot_in, device):
        return pltpu.make_async_remote_copy(
            src_ref=src,
            dst_ref=dst,
            send_sem=sems.at[0, slot_out],
            recv_sem=sems.at[1, slot_in],
            device_id=device,
            device_id_type=MESH,
        )

    def send(src, dst, sems, slot_out, slot_in, device):
        copy = remote(src, dst, sems, slot_out, slot_in, device)
        copy.start()
        sent.append(copy)

    def arrived(dst, sems, slot_in):
        remote(dst, dst, sems, slot_in, slot_in, sibling).wait_recv()

    first = lax.broadcasted_iota(jnp.int32, (1, PAIR), 1) < HEAD
    rows = lax.broadcasted_iota(jnp.int32, (TOKENS, TOKENS), 0)
    cols = lax.broadcasted_iota(jnp.int32, (TOKENS, TOKENS), 1)
    triangle = jnp.where(rows <= cols, 1.0, 0.0).astype(BF16)
    load_decay.wait()
    sums = dot(split3(decay[...]).astype(BF16), triangle)
    turned = sums[:HEADS] + (sums[HEADS : 2 * HEADS] + sums[2 * HEADS :])
    for h in range(HEADS):
        cum_t[h] = turned[h : h + 1, :]
    falls = jnp.exp(jnp.broadcast_to(turned[:, TOKENS - 1 :], (HEADS, PAIR)))
    for p in range(PAIRS):
        f_own[p : p + 1, :] = jnp.where(
            first, falls[2 * p : 2 * p + 1], falls[2 * p + 1 : 2 * p + 2]
        )
    padded = jnp.concatenate(
        [split3(turned), jnp.zeros((PAIR - 3 * HEADS, TOKENS), F32)], axis=0
    )
    upright = padded.T.astype(BF16)

    def project_states(n):
        quad = order[n]
        r = lax.broadcasted_iota(jnp.int32, (PAIR, 4 * PAIR), 0)
        s = lax.broadcasted_iota(jnp.int32, (PAIR, 4 * PAIR), 1)
        spread = jnp.where((r % HEADS == quad * 4 + s // PAIR) & (r < 3 * HEADS), 1.0, 0.0)
        cums = dot(upright, spread.astype(BF16))
        keys = silu(dot(tok[...], wk[n])).astype(BF16)
        values = dot(tok[...], wv[n]).astype(BF16)
        for e in range(2):
            p = 2 * quad + e
            part = slice(e * PAIR, (e + 1) * PAIR)
            one = cums[:, 2 * e * PAIR : (2 * e + 1) * PAIR]
            two = cums[:, (2 * e + 1) * PAIR : (2 * e + 2) * PAIR]
            cum_b[2 * p] = one
            cum_b[2 * p + 1] = two
            k[p] = keys[:, part]
            v[p] = values[:, part]
            run = jnp.where(first, one, two)
            left = jnp.exp(run[TOKENS - 1 :, :] - run)
            scaled = (keys[:, part].astype(F32) * left).astype(BF16)
            outer = dot_tn(scaled, values[:, part])
            own = jnp.where(first, outer[:HEAD], outer[HEAD:])
            local[p] = own.reshape(2, HALF, PAIR)

    def send_cross(n):
        two = pl.ds(2 * order[n], 2)
        send(local.at[two, 1 - c], crossed.at[two], s0_sem, n, n, sibling)

    def exchange_falls():
        arrived(f_sib, f0_sem, 0)
        both = f_own[...] * f_sib[...]
        f_chip[...] = both
        f_in1[z] = both
        for d in far_z:
            send(f_chip, f_in1.at[z], f1_sem, d, z, at_z(along(d)))

    def send_chip(n):
        two = pl.ds(2 * order[n], 2)
        arrived(crossed.at[two], s0_sem, n)
        for e in range(2):
            p = 2 * order[n] + e
            own = local[p, c]
            other = crossed[p]
            late = jnp.where(c == 0, f_sib[pl.ds(p, 1), :], f_own[pl.ds(p, 1), :])
            chip[p] = jnp.where(c == 0, late * own + other, late * other + own)
        if n < QUADS - 1:
            for e in range(2):
                p = 2 * order[n] + e
                send(chip.at[p], in1.at[z], s1_sem, 2 * n + e, z, at_z(p))
        else:
            in1[z] = chip[z]
            p = z + 1 - 2 * odd
            send(chip.at[p], in1.at[z], s1_sem, 2 * n, z, at_z(p))

    def project_queries(n):
        load_q[n].wait()
        queries = silu(dot(tok[...], wq[n])).astype(BF16)
        q[2 * n] = queries[:, :PAIR]
        q[2 * n + 1] = queries[:, PAIR:]

    def attend(p):
        for i in range(TOKENS // SUB):
            here = slice(i * SUB, (i + 1) * SUB)
            upto = (i + 1) * SUB
            queries = q[p, here, :]
            nothing = jnp.zeros_like(queries)
            keys = k[p, :upto, :]
            weights = []
            for e in range(2):
                own = (
                    jnp.where(first, queries, nothing)
                    if e == 0
                    else jnp.where(first, nothing, queries)
                )
                scores = dot_nt(own, keys)
                row = cum_b[2 * p + e, here, :]
                for j in range(i + 1):
                    diff = row - cum_t[2 * p + e, :, j * SUB : (j + 1) * SUB]
                    if j == i:
                        r = lax.broadcasted_iota(jnp.int32, (SUB, SUB), 0)
                        s = lax.broadcasted_iota(jnp.int32, (SUB, SUB), 1)
                        diff = jnp.where(s <= r, diff, -jnp.inf)
                    weights.append(
                        (scores[:, j * SUB : (j + 1) * SUB] * jnp.exp(diff)).astype(BF16)
                    )
            values = v[p, :upto, :]
            nothing = jnp.zeros_like(values)
            heads = jnp.concatenate(
                [jnp.where(first, values, nothing), jnp.where(first, nothing, values)], axis=0
            )
            intra[p, here, :] = dot(jnp.concatenate(weights, axis=1), heads)

    load_tok.wait()
    for n in range(QUADS):
        load_k[n].wait()
        load_v[n].wait()
        project_states(n)
        if n == 0:
            pl.semaphore_wait(barrier, chips + outers - 1)
            send(f_own, f_sib, f0_sem, 0, 0, sibling)
        send_cross(n)
        if n == 1:
            exchange_falls()
        if n >= 1:
            send_chip(n - 1)
    project_queries(0)
    send_chip(QUADS - 1)
    for n in range(1, QUADS):
        project_queries(n)
    for p in range(0, 2):
        attend(p)

    for d in near_z[1:]:
        arrived(f_in1.at[along(d)], f1_sem, along(d))
        arrived(in1.at[along(d)], s1_sem, along(d))
    run = jnp.zeros((HALF, PAIR), F32)
    group = jnp.ones((1, PAIR), F32)
    for i in range(chips):
        prefix[i] = run
        fall = f_in1[i, pl.ds(z, 1), :]
        run = fall * run + in1[i]
        group = group * fall
    total[:HALF] = run
    total[HALF:] = jnp.broadcast_to(group, (8, PAIR))
    for n, (a, b) in enumerate(plane):
        other = group_at(a, b)

        @pl.when(other > o)
        def _():
            remote(total, in2.at[o], s2_sem, n, o, (other, inner)).start()

    for p in range(2, 7):
        attend(p)

    def earlier(i, before):
        arrived(in2.at[i], s2_sem, i)
        return in2[i, HALF : HALF + 1, :] * before + in2[i, :HALF, :]

    before = lax.fori_loop(0, o, earlier, jnp.zeros((HALF, PAIR), F32))
    fall = jnp.ones((1, PAIR), F32)
    for i in range(chips):
        out3[i] = fall * before + prefix[i]
        fall = fall * f_in1[i, pl.ds(z, 1), :]
    for d in far_z:
        t = along(d)
        send(out3.at[t], in3.at[z], s3_sem, d, z, at_z(t))
    in3[z] = out3[z]

    for p in range(7, PAIRS):
        attend(p)
    load_gain.wait()
    for n in range(PAIRS):
        load_o[n].wait()

    def enter(d):
        p = along(d)
        if d > 0:
            arrived(in3.at[p], s3_sem, p)
        enters = in3[p]
        first_local = jnp.where(c == 0, local[p, 0], crossed[p])
        fall = jnp.where(c == 0, f_own[pl.ds(p, 1), :], f_sib[pl.ds(p, 1), :])
        middle = fall * enters + first_local
        state[p, c] = jnp.where(c == 0, enters, middle)
        give[p] = jnp.where(c == 0, middle, enters)
        send(give.at[p], state.at[p, c], s4_sem, p, p, sibling)

    r = lax.broadcasted_iota(jnp.int32, (PAIR, PAIR), 0) // HEAD
    s = lax.broadcasted_iota(jnp.int32, (PAIR, PAIR), 1) // HEAD
    means = jnp.where(r == s, 1.0 / HEAD, 0.0).astype(BF16)

    def norm(pairs):
        for p in pairs:
            arrived(state.at[p, 1 - c], s4_sem, p)
        for p in pairs:
            flat = state[p].reshape(HEAD, PAIR)
            both = jnp.concatenate(
                [jnp.where(first, flat, 0.0), jnp.where(first, 0.0, flat)], axis=0
            )
            inter = dot(q[p], both.astype(BF16))
            run = jnp.where(first, cum_b[2 * p], cum_b[2 * p + 1])
            attended = intra[p] + jnp.exp(run) * inter
            mean = dot((attended * attended).astype(BF16), means)
            normed[p] = (attended * lax.rsqrt(mean + 1e-5) * gain[p]).astype(BF16)

    def mix(pairs, n):
        left = jnp.concatenate([normed[p] for p in pairs], axis=1)
        right = jnp.concatenate([wo[p, :, n * QUAD : (n + 1) * QUAD] for p in pairs], axis=0)
        return dot(left, right)

    near = [along(d) for d in near_z[:5]]
    far = [along(d) for d in near_z[5:]]
    for d in near_z[:5]:
        enter(d)
    norm(near)
    for d in near_z[5:]:
        enter(d)
    for n in range(QUADS):
        partial[n] = mix(near, n)
    norm(far)
    stores = []
    for n in range(QUADS):
        out[n] = (partial[n] + mix(far, n)).astype(BF16)
        copy = pltpu.make_async_copy(
            out.at[n], out_hbm.at[:, pl.ds(n * QUAD, QUAD)], store_sem.at[n]
        )
        copy.start()
        stores.append(copy)

    for copy in sent:
        copy.wait_send()
    for n, (a, b) in enumerate(plane):

        @pl.when(group_at(a, b) > o)
        def _():
            remote(total, total, s2_sem, n, n, sibling).wait_send()

    for copy in stores:
        copy.wait()


MESH = pl.DeviceIdType.MESH


def solution(mesh):
    outers, chips = mesh.shape["outer"], mesh.shape["inner"] // 2

    def shards(tokens, log_decay, query_weight, key_weight, value_weight, norm_gain, output_weight):
        vmem = pltpu.VMEM
        dma = pltpu.SemaphoreType.DMA
        weight = vmem((QUADS, WIDTH, QUAD), BF16)
        by_pair = vmem((PAIRS, TOKENS, PAIR), BF16)
        unit = (HALF, PAIR)
        tile = (PAIRS, PAIR)
        return pl.pallas_call(
            functools.partial(kernel, outers, chips),
            out_shape=jax.ShapeDtypeStruct((TOKENS, WIDTH), BF16),
            in_specs=[pl.BlockSpec(memory_space=pl.ANY)] * 7,
            out_specs=pl.BlockSpec(memory_space=pl.ANY),
            scratch_shapes=[
                vmem((TOKENS, WIDTH), BF16),
                vmem((HEADS, TOKENS), F32),
                weight,
                weight,
                weight,
                vmem((PAIRS, 1, PAIR), F32),
                vmem((PAIRS, PAIR, WIDTH), BF16),
                by_pair,
                by_pair,
                by_pair,
                vmem((HEADS, TOKENS, PAIR), F32),
                vmem((HEADS, 1, TOKENS), F32),
                vmem((PAIRS, TOKENS, PAIR), F32),
                vmem((PAIRS, 2) + unit, F32),
                vmem((PAIRS,) + unit, F32),
                vmem((PAIRS,) + unit, F32),
                vmem((chips,) + unit, F32),
                vmem((chips,) + unit, F32),
                vmem((HALF + 8, PAIR), F32),
                vmem((outers, HALF + 8, PAIR), F32),
                vmem((chips,) + unit, F32),
                vmem((PAIRS,) + unit, F32),
                vmem((PAIRS,) + unit, F32),
                vmem((PAIRS, 2) + unit, F32),
                vmem(tile, F32),
                vmem(tile, F32),
                vmem(tile, F32),
                vmem((chips,) + tile, F32),
                by_pair,
                vmem((QUADS, TOKENS, QUAD), F32),
                vmem((QUADS, TOKENS, QUAD), BF16),
                dma((23,)),
                dma((QUADS,)),
                dma((2, 1)),
                dma((2, chips)),
                dma((2, QUADS)),
                dma((2, chips)),
                dma((2, outers)),
                dma((2, chips)),
                dma((2, PAIRS)),
            ],
            compiler_params=pltpu.CompilerParams(
                collective_id=0, has_side_effects=True, vmem_limit_bytes=62 << 20
            ),
            cost_estimate=pl.CostEstimate(
                flops=4 * 10**9, bytes_accessed=10 << 20, transcendentals=2 * 10**6
            ),
        )(
            tokens,
            log_decay.T,
            query_weight,
            key_weight,
            value_weight,
            norm_gain.reshape(PAIRS, 1, PAIR),
            output_weight,
        )

    in_specs = (P(("outer", "inner"), None), P(("outer", "inner"), None), P(), P(), P(), P(), P())
    out_specs = P(("outer", "inner"), None)
    return jax.shard_map(shards, mesh=mesh, in_specs=in_specs, out_specs=out_specs, check_vma=False)
```

```python
import functools

import jax
import jax.numpy as jnp
from jax import lax
from jax.experimental import pallas as pl
from jax.experimental.pallas import tpu as pltpu
from jax.sharding import PartitionSpec as P

F32 = jnp.float32
BF16 = jnp.bfloat16
HEADS = 16
HEAD = 64
PAIRS = 8
PAIR = 128
QUADS = 4
QUAD = 256
TOKENS = 384
SUB = 128
WIDTH = 1024
BARRIER = 2
SIDE = 4
HALF = 32


def dot(a, b):
    return jnp.dot(a, b, preferred_element_type=F32)


def dot_nt(a, b):
    return lax.dot_general(a, b, (((1,), (1,)), ((), ())), preferred_element_type=F32)


def dot_tn(a, b):
    return lax.dot_general(a, b, (((0,), (0,)), ((), ())), preferred_element_type=F32)


def silu(x):
    return x * (0.5 * jnp.tanh(0.5 * x) + 0.5)


def split3(x):
    hi = x.astype(BF16).astype(F32)
    rest = x - hi
    mid = rest.astype(BF16).astype(F32)
    return jnp.concatenate([hi, mid, rest - mid], axis=0)


def kernel(
    outers,
    chips,
    tok_hbm,
    decay_hbm,
    wq_hbm,
    wk_hbm,
    wv_hbm,
    gain_hbm,
    wo_hbm,
    out_hbm,
    tok,
    decay,
    wq,
    wk,
    wv,
    gain,
    wo,
    q,
    k,
    v,
    cum_b,
    cum_t,
    intra,
    local,
    crossed,
    chip,
    in1,
    prefix,
    total,
    in2,
    out3,
    in3,
    give,
    state,
    f_own,
    f_sib,
    f_chip,
    normed,
    partial,
    out,
    load_sem,
    store_sem,
    f0_sem,
    s0_sem,
    s1_sem,
    s2_sem,
    s3_sem,
    s4_sem,
):
    o = lax.axis_index("outer")
    inner = lax.axis_index("inner")
    z, c = inner // 2, inner % 2
    y, x = o // SIDE, o % SIDE
    sibling = (o, z * 2 + 1 - c)

    def along(d):
        return (z + d) % chips

    def at_z(other):
        return (o, other * 2 + c)

    far_z = sorted(range(1, chips), key=lambda d: -min(d, chips - d))
    near_z = [0] + far_z[::-1]
    plane = sorted(
        ((a, b) for a in range(outers // SIDE) for b in range(SIDE) if (a, b) != (0, 0)),
        key=lambda t: -(min(t[0], outers // SIDE - t[0]) + min(t[1], SIDE - t[1])),
    )

    def group_at(a, b):
        return (y + a) % (outers // SIDE) * SIDE + (x + b) % SIDE

    def load(src, dst, n):
        copy = pltpu.make_async_copy(src, dst, load_sem.at[n])
        copy.start()
        return copy

    mine = z // 2
    odd = z % 2
    order = [(mine + 2) % QUADS, (mine + 1 + 2 * odd) % QUADS, (mine + 3 - 2 * odd) % QUADS, mine]

    load_decay = load(decay_hbm, decay, 0)
    load_tok = load(tok_hbm, tok, 1)
    load_k, load_v = [], []

    def load_quad(n):
        cols = pl.ds(pl.multiple_of(order[n] * QUAD, QUAD), QUAD)
        load_k.append(load(wk_hbm.at[:, cols], wk.at[n], 2 + n))
        load_v.append(load(wv_hbm.at[:, cols], wv.at[n], 6 + n))

    load_quad(0)

    barrier = pltpu.get_barrier_semaphore()
    for d in far_z:
        pl.semaphore_signal(barrier, inc=1, device_id=at_z(along(d)), device_id_type=MESH)
    pl.semaphore_signal(barrier, inc=1, device_id=sibling, device_id_type=MESH)
    load_quad(1)
    for a, b in plane:
        other = group_at(a, b)

        @pl.when(other < o)
        def _():
            pl.semaphore_signal(barrier, inc=1, device_id=(other, inner), device_id_type=MESH)

    for n in range(2, QUADS):
        load_quad(n)

    load_q = load(wq_hbm, wq, 10)
    load_o = load(wo_hbm, wo, 11)
    load_gain = load(gain_hbm, gain, 12)

    sent = []

    def settle():
        for copy in sent:
            copy.wait_send()
        sent.clear()

    def remote(src, dst, sems, slot_out, slot_in, device):
        return pltpu.make_async_remote_copy(
            src_ref=src,
            dst_ref=dst,
            send_sem=sems.at[0, slot_out],
            recv_sem=sems.at[1, slot_in],
            device_id=device,
            device_id_type=MESH,
        )

    def send(src, dst, sems, slot_out, slot_in, device):
        copy = remote(src, dst, sems, slot_out, slot_in, device)
        copy.start()
        sent.append(copy)

    def arrived(dst, sems, slot_in):
        remote(dst, dst, sems, slot_in, slot_in, sibling).wait_recv()

    first = lax.broadcasted_iota(jnp.int32, (1, PAIR), 1) < HEAD
    rows = lax.broadcasted_iota(jnp.int32, (TOKENS, TOKENS), 0)
    cols = lax.broadcasted_iota(jnp.int32, (TOKENS, TOKENS), 1)
    triangle = jnp.where(rows <= cols, 1.0, 0.0).astype(BF16)
    load_decay.wait()
    sums = dot(split3(decay[...]).astype(BF16), triangle)
    turned = sums[:HEADS] + (sums[HEADS : 2 * HEADS] + sums[2 * HEADS :])
    for h in range(HEADS):
        cum_t[h] = turned[h : h + 1, :]
    falls = jnp.exp(jnp.broadcast_to(turned[:, TOKENS - 1 :], (HEADS, PAIR)))
    for p in range(PAIRS):
        f_own[p : p + 1, :] = jnp.where(
            first, falls[2 * p : 2 * p + 1], falls[2 * p + 1 : 2 * p + 2]
        )
    padded = jnp.concatenate(
        [split3(turned), jnp.zeros((PAIR - 3 * HEADS, TOKENS), F32)], axis=0
    )
    upright = padded.T.astype(BF16)

    def project_states(n):
        quad = order[n]
        r = lax.broadcasted_iota(jnp.int32, (PAIR, 4 * PAIR), 0)
        s = lax.broadcasted_iota(jnp.int32, (PAIR, 4 * PAIR), 1)
        spread = jnp.where((r % HEADS == quad * 4 + s // PAIR) & (r < 3 * HEADS), 1.0, 0.0)
        cums = dot(upright, spread.astype(BF16))
        keys = silu(dot(tok[...], wk[n])).astype(BF16)
        values = dot(tok[...], wv[n]).astype(BF16)
        for e in range(2):
            p = 2 * quad + e
            part = slice(e * PAIR, (e + 1) * PAIR)
            one = cums[:, 2 * e * PAIR : (2 * e + 1) * PAIR]
            two = cums[:, (2 * e + 1) * PAIR : (2 * e + 2) * PAIR]
            cum_b[2 * p] = one
            cum_b[2 * p + 1] = two
            k[p] = keys[:, part]
            v[p] = values[:, part]
            run = jnp.where(first, one, two)
            left = jnp.exp(run[TOKENS - 1 :, :] - run)
            scaled = (keys[:, part].astype(F32) * left).astype(BF16)
            outer = dot_tn(scaled, values[:, part])
            own = jnp.where(first, outer[:HEAD], outer[HEAD:])
            local[p] = own.reshape(2, HALF, PAIR)

    def send_cross(n):
        two = pl.ds(2 * order[n], 2)
        send(local.at[two, 1 - c], crossed.at[two], s0_sem, n, n, sibling)

    def exchange_falls():
        arrived(f_sib, f0_sem, 0)
        f_chip[...] = f_own[...] * f_sib[...]

    def send_chip(n):
        two = pl.ds(2 * order[n], 2)
        arrived(crossed.at[two], s0_sem, n)
        for e in range(2):
            p = 2 * order[n] + e
            own = local[p, c]
            other = crossed[p]
            late = jnp.where(c == 0, f_sib[pl.ds(p, 1), :], f_own[pl.ds(p, 1), :])
            chip[p, :HALF] = jnp.where(c == 0, late * own + other, late * other + own)
            chip[p, HALF:] = jnp.broadcast_to(f_chip[pl.ds(p, 1), :], (8, PAIR))
        if n < QUADS - 1:
            for e in range(2):
                p = 2 * order[n] + e
                send(chip.at[p], in1.at[z], s1_sem, 2 * n + e, z, at_z(p))
        else:
            in1[z] = chip[z]
            p = z + 1 - 2 * odd
            send(chip.at[p], in1.at[z], s1_sem, 2 * n, z, at_z(p))

    def project_queries(n):
        queries = silu(dot(tok[...], wq[:, n * QUAD : (n + 1) * QUAD])).astype(BF16)
        q[2 * n] = queries[:, :PAIR]
        q[2 * n + 1] = queries[:, PAIR:]

    def attend(p):
        for i in range(TOKENS // SUB):
            here = slice(i * SUB, (i + 1) * SUB)
            upto = (i + 1) * SUB
            queries = q[p, here, :]
            nothing = jnp.zeros_like(queries)
            keys = k[p, :upto, :]
            weights = []
            for e in range(2):
                own = (
                    jnp.where(first, queries, nothing)
                    if e == 0
                    else jnp.where(first, nothing, queries)
                )
                scores = dot_nt(own, keys)
                row = cum_b[2 * p + e, here, :]
                for j in range(i + 1):
                    diff = row - cum_t[2 * p + e, :, j * SUB : (j + 1) * SUB]
                    if j == i:
                        r = lax.broadcasted_iota(jnp.int32, (SUB, SUB), 0)
                        s = lax.broadcasted_iota(jnp.int32, (SUB, SUB), 1)
                        diff = jnp.where(s <= r, diff, -jnp.inf)
                    weights.append(
                        (scores[:, j * SUB : (j + 1) * SUB] * jnp.exp(diff)).astype(BF16)
                    )
            values = v[p, :upto, :]
            nothing = jnp.zeros_like(values)
            heads = jnp.concatenate(
                [jnp.where(first, values, nothing), jnp.where(first, nothing, values)], axis=0
            )
            intra[p, here, :] = dot(jnp.concatenate(weights, axis=1), heads)

    load_tok.wait()
    for n in range(QUADS):
        load_k[n].wait()
        load_v[n].wait()
        project_states(n)
        if n == BARRIER:
            pl.semaphore_wait(barrier, chips + outers - 1 - o)
            send(f_own, f_sib, f0_sem, 0, 0, sibling)
            for m in range(n):
                send_cross(m)
        if n >= BARRIER:
            send_cross(n)
        if n == BARRIER + 1:
            exchange_falls()
            for m in range(BARRIER):
                send_chip(m)
        if n >= BARRIER + 1:
            send_chip(n - 1)
    load_q.wait()
    project_queries(0)
    send_chip(QUADS - 1)
    for n in range(1, QUADS):
        project_queries(n)
    for p in range(0, 2):
        attend(p)

    for d in near_z[1:]:
        arrived(in1.at[along(d)], s1_sem, along(d))
    run = jnp.zeros((HALF, PAIR), F32)
    group = jnp.ones((1, PAIR), F32)
    for i in range(chips):
        prefix[i] = run
        fall = in1[i, HALF : HALF + 1, :]
        run = fall * run + in1[i, :HALF, :]
        group = group * fall
    total[:HALF] = run
    total[HALF:] = jnp.broadcast_to(group, (8, PAIR))
    for n, (a, b) in enumerate(plane):
        other = group_at(a, b)

        @pl.when(other > o)
        def _():
            remote(total, in2.at[o], s2_sem, n, o, (other, inner)).start()

    settle()
    for p in range(2, 7):
        attend(p)

    def earlier(i, before):
        arrived(in2.at[i], s2_sem, i)
        return in2[i, HALF : HALF + 1, :] * before + in2[i, :HALF, :]

    before = lax.fori_loop(0, o, earlier, jnp.zeros((HALF, PAIR), F32))
    fall = jnp.ones((1, PAIR), F32)
    for i in range(chips):
        out3[i] = fall * before + prefix[i]
        fall = fall * in1[i, HALF : HALF + 1, :]
    for d in far_z:
        t = along(d)
        send(out3.at[t], in3.at[z], s3_sem, d, z, at_z(t))
    in3[z] = out3[z]

    for p in range(7, PAIRS):
        attend(p)
    settle()
    for n, (a, b) in enumerate(plane):

        @pl.when(group_at(a, b) > o)
        def _():
            remote(total, total, s2_sem, n, n, sibling).wait_send()

    load_gain.wait()
    load_o.wait()

    def enter(d):
        p = along(d)
        if d > 0:
            arrived(in3.at[p], s3_sem, p)
        enters = in3[p]
        first_local = jnp.where(c == 0, local[p, 0], crossed[p])
        fall = jnp.where(c == 0, f_own[pl.ds(p, 1), :], f_sib[pl.ds(p, 1), :])
        middle = fall * enters + first_local
        state[p, c] = jnp.where(c == 0, enters, middle)
        give[p] = jnp.where(c == 0, middle, enters)
        send(give.at[p], state.at[p, c], s4_sem, p, p, sibling)

    r = lax.broadcasted_iota(jnp.int32, (PAIR, PAIR), 0) // HEAD
    s = lax.broadcasted_iota(jnp.int32, (PAIR, PAIR), 1) // HEAD
    means = jnp.where(r == s, 1.0 / HEAD, 0.0).astype(BF16)

    def norm(pairs):
        for p in pairs:
            arrived(state.at[p, 1 - c], s4_sem, p)
        for p in pairs:
            flat = state[p].reshape(HEAD, PAIR)
            both = jnp.concatenate(
                [jnp.where(first, flat, 0.0), jnp.where(first, 0.0, flat)], axis=0
            )
            inter = dot(q[p], both.astype(BF16))
            run = jnp.where(first, cum_b[2 * p], cum_b[2 * p + 1])
            attended = intra[p] + jnp.exp(run) * inter
            mean = dot((attended * attended).astype(BF16), means)
            normed[p] = (attended * lax.rsqrt(mean + 1e-5) * gain[p]).astype(BF16)

    def mix(pairs, n):
        left = jnp.concatenate([normed[p] for p in pairs], axis=1)
        right = jnp.concatenate([wo[p, :, n * QUAD : (n + 1) * QUAD] for p in pairs], axis=0)
        return dot(left, right)

    near = [along(d) for d in near_z[:6]]
    far = [along(d) for d in near_z[6:]]
    for d in near_z[:6]:
        enter(d)
    norm(near)
    for d in near_z[6:]:
        enter(d)
    for n in range(QUADS):
        partial[n] = mix(near, n)
    norm(far)
    stores = []
    for n in range(QUADS):
        out[n] = (partial[n] + mix(far, n)).astype(BF16)
        copy = pltpu.make_async_copy(
            out.at[n], out_hbm.at[:, pl.ds(n * QUAD, QUAD)], store_sem.at[n]
        )
        copy.start()
        stores.append(copy)

    settle()
    for copy in stores:
        copy.wait()


MESH = pl.DeviceIdType.MESH


def solution(mesh):
    outers, chips = mesh.shape["outer"], mesh.shape["inner"] // 2

    def shards(tokens, log_decay, query_weight, key_weight, value_weight, norm_gain, output_weight):
        vmem = pltpu.VMEM
        dma = pltpu.SemaphoreType.DMA
        weight = vmem((QUADS, WIDTH, QUAD), BF16)
        by_pair = vmem((PAIRS, TOKENS, PAIR), BF16)
        unit = (HALF, PAIR)
        tile = (PAIRS, PAIR)
        return pl.pallas_call(
            functools.partial(kernel, outers, chips),
            out_shape=jax.ShapeDtypeStruct((TOKENS, WIDTH), BF16),
            in_specs=[pl.BlockSpec(memory_space=pl.ANY)] * 7,
            out_specs=pl.BlockSpec(memory_space=pl.ANY),
            scratch_shapes=[
                vmem((TOKENS, WIDTH), BF16),
                vmem((HEADS, TOKENS), F32),
                vmem((WIDTH, WIDTH), BF16),
                weight,
                weight,
                vmem((PAIRS, 1, PAIR), F32),
                vmem((PAIRS, PAIR, WIDTH), BF16),
                by_pair,
                by_pair,
                by_pair,
                vmem((HEADS, TOKENS, PAIR), F32),
                vmem((HEADS, 1, TOKENS), F32),
                vmem((PAIRS, TOKENS, PAIR), F32),
                vmem((PAIRS, 2) + unit, F32),
                vmem((PAIRS,) + unit, F32),
                vmem((PAIRS, HALF + 8, PAIR), F32),
                vmem((chips, HALF + 8, PAIR), F32),
                vmem((chips,) + unit, F32),
                vmem((HALF + 8, PAIR), F32),
                vmem((outers, HALF + 8, PAIR), F32),
                vmem((chips,) + unit, F32),
                vmem((PAIRS,) + unit, F32),
                vmem((PAIRS,) + unit, F32),
                vmem((PAIRS, 2) + unit, F32),
                vmem(tile, F32),
                vmem(tile, F32),
                vmem(tile, F32),
                by_pair,
                vmem((QUADS, TOKENS, QUAD), F32),
                vmem((QUADS, TOKENS, QUAD), BF16),
                dma((13,)),
                dma((QUADS,)),
                dma((2, 1)),
                dma((2, QUADS)),
                dma((2, chips)),
                dma((2, outers)),
                dma((2, chips)),
                dma((2, PAIRS)),
            ],
            compiler_params=pltpu.CompilerParams(
                collective_id=0, has_side_effects=True, vmem_limit_bytes=62 << 20
            ),
            cost_estimate=pl.CostEstimate(
                flops=4 * 10**9, bytes_accessed=10 << 20, transcendentals=2 * 10**6
            ),
        )(
            tokens,
            log_decay.T,
            query_weight,
            key_weight,
            value_weight,
            norm_gain.reshape(PAIRS, 1, PAIR),
            output_weight.reshape(PAIRS, PAIR, WIDTH),
        )

    in_specs = (P(("outer", "inner"), None), P(("outer", "inner"), None), P(), P(), P(), P(), P())
    out_specs = P(("outer", "inner"), None)
    return jax.shard_map(shards, mesh=mesh, in_specs=in_specs, out_specs=out_specs, check_vma=False)
```

```python
import functools

import jax
import jax.numpy as jnp
from jax import lax
from jax.experimental import pallas as pl
from jax.experimental.pallas import tpu as pltpu
from jax.sharding import PartitionSpec as P

F32 = jnp.float32
BF16 = jnp.bfloat16
HEADS = 16
HEAD = 64
PAIRS = 8
PAIR = 128
QUADS = 4
QUAD = 256
TOKENS = 384
SUB = 128
WIDTH = 1024
BARRIER = 2
SIDE = 4
HALF = 32


def dot(a, b):
    return jnp.dot(a, b, preferred_element_type=F32)


def dot_nt(a, b):
    return lax.dot_general(a, b, (((1,), (1,)), ((), ())), preferred_element_type=F32)


def dot_tn(a, b):
    return lax.dot_general(a, b, (((0,), (0,)), ((), ())), preferred_element_type=F32)


def silu(x):
    return x * (0.5 * jnp.tanh(0.5 * x) + 0.5)


def split3(x):
    hi = x.astype(BF16).astype(F32)
    rest = x - hi
    mid = rest.astype(BF16).astype(F32)
    return jnp.concatenate([hi, mid, rest - mid], axis=0)


def kernel(
    outers,
    chips,
    tok_hbm,
    decay_hbm,
    wq_hbm,
    wk_hbm,
    wv_hbm,
    gain_hbm,
    wo_hbm,
    out_hbm,
    tok,
    decay,
    wq,
    wk,
    wv,
    gain,
    wo,
    q,
    k,
    v,
    cum_b,
    cum_t,
    intra,
    local,
    crossed,
    chip,
    in1,
    prefix,
    total,
    in2,
    out3,
    in3,
    give,
    state,
    f_own,
    f_sib,
    f_chip,
    normed,
    partial,
    out,
    load_sem,
    store_sem,
    f0_sem,
    s0_sem,
    s1_sem,
    s2_sem,
    s3_sem,
    s4_sem,
):
    o = lax.axis_index("outer")
    inner = lax.axis_index("inner")
    z, c = inner // 2, inner % 2
    y, x = o // SIDE, o % SIDE
    sibling = (o, z * 2 + 1 - c)

    def along(d):
        return (z + d) % chips

    def at_z(other):
        return (o, other * 2 + c)

    far_z = sorted(range(1, chips), key=lambda d: -min(d, chips - d))
    near_z = [0] + far_z[::-1]
    plane = sorted(
        ((a, b) for a in range(outers // SIDE) for b in range(SIDE) if (a, b) != (0, 0)),
        key=lambda t: -(min(t[0], outers // SIDE - t[0]) + min(t[1], SIDE - t[1])),
    )

    def group_at(a, b):
        return (y + a) % (outers // SIDE) * SIDE + (x + b) % SIDE

    def load(src, dst, n):
        copy = pltpu.make_async_copy(src, dst, load_sem.at[n])
        copy.start()
        return copy

    mine = z // 2
    odd = z % 2
    order = [(mine + 2) % QUADS, (mine + 1 + 2 * odd) % QUADS, (mine + 3 - 2 * odd) % QUADS, mine]

    barrier = pltpu.get_barrier_semaphore()
    for d in far_z:
        pl.semaphore_signal(barrier, inc=1, device_id=at_z(along(d)), device_id_type=MESH)
    pl.semaphore_signal(barrier, inc=1, device_id=sibling, device_id_type=MESH)
    load_decay = load(decay_hbm, decay, 0)
    load_tok = load(tok_hbm, tok, 1)
    load_k, load_v = [], []

    def load_quad(n):
        cols = pl.ds(pl.multiple_of(order[n] * QUAD, QUAD), QUAD)
        load_k.append(load(wk_hbm.at[:, cols], wk.at[n], 2 + n))
        load_v.append(load(wv_hbm.at[:, cols], wv.at[n], 6 + n))

    load_quad(0)

    load_quad(1)
    for a, b in plane:
        other = group_at(a, b)

        @pl.when(other < o)
        def _():
            pl.semaphore_signal(barrier, inc=1, device_id=(other, inner), device_id_type=MESH)

    for n in range(2, QUADS):
        load_quad(n)

    load_q = load(wq_hbm, wq, 10)
    load_o = load(wo_hbm, wo, 11)
    load_gain = load(gain_hbm, gain, 12)

    sent = []

    def settle():
        for copy in sent:
            copy.wait_send()
        sent.clear()

    def remote(src, dst, sems, slot_out, slot_in, device):
        return pltpu.make_async_remote_copy(
            src_ref=src,
            dst_ref=dst,
            send_sem=sems.at[0, slot_out],
            recv_sem=sems.at[1, slot_in],
            device_id=device,
            device_id_type=MESH,
        )

    def send(src, dst, sems, slot_out, slot_in, device):
        copy = remote(src, dst, sems, slot_out, slot_in, device)
        copy.start()
        sent.append(copy)

    def arrived(dst, sems, slot_in):
        remote(dst, dst, sems, slot_in, slot_in, sibling).wait_recv()

    first = lax.broadcasted_iota(jnp.int32, (1, PAIR), 1) < HEAD
    rows = lax.broadcasted_iota(jnp.int32, (TOKENS, TOKENS), 0)
    cols = lax.broadcasted_iota(jnp.int32, (TOKENS, TOKENS), 1)
    triangle = jnp.where(rows <= cols, 1.0, 0.0).astype(BF16)
    load_decay.wait()
    sums = dot(split3(decay[...]).astype(BF16), triangle)
    turned = sums[:HEADS] + (sums[HEADS : 2 * HEADS] + sums[2 * HEADS :])
    for h in range(HEADS):
        cum_t[h] = turned[h : h + 1, :]
    falls = jnp.exp(jnp.broadcast_to(turned[:, TOKENS - 1 :], (HEADS, PAIR)))
    for p in range(PAIRS):
        f_own[p : p + 1, :] = jnp.where(
            first, falls[2 * p : 2 * p + 1], falls[2 * p + 1 : 2 * p + 2]
        )
    padded = jnp.concatenate(
        [split3(turned), jnp.zeros((PAIR - 3 * HEADS, TOKENS), F32)], axis=0
    )
    upright = padded.T.astype(BF16)

    def project_states(n):
        quad = order[n]
        r = lax.broadcasted_iota(jnp.int32, (PAIR, 4 * PAIR), 0)
        s = lax.broadcasted_iota(jnp.int32, (PAIR, 4 * PAIR), 1)
        spread = jnp.where((r % HEADS == quad * 4 + s // PAIR) & (r < 3 * HEADS), 1.0, 0.0)
        cums = dot(upright, spread.astype(BF16))
        keys = silu(dot(tok[...], wk[n])).astype(BF16)
        values = dot(tok[...], wv[n]).astype(BF16)
        for e in range(2):
            p = 2 * quad + e
            part = slice(e * PAIR, (e + 1) * PAIR)
            one = cums[:, 2 * e * PAIR : (2 * e + 1) * PAIR]
            two = cums[:, (2 * e + 1) * PAIR : (2 * e + 2) * PAIR]
            cum_b[2 * p] = one
            cum_b[2 * p + 1] = two
            k[p] = keys[:, part]
            v[p] = values[:, part]
            run = jnp.where(first, one, two)
            left = jnp.exp(run[TOKENS - 1 :, :] - run)
            scaled = (keys[:, part].astype(F32) * left).astype(BF16)
            outer = dot_tn(scaled, values[:, part])
            own = jnp.where(first, outer[:HEAD], outer[HEAD:])
            local[p] = own.reshape(2, HALF, PAIR)

    def send_cross(n):
        two = pl.ds(2 * order[n], 2)
        send(local.at[two, 1 - c], crossed.at[two], s0_sem, n, n, sibling)

    def exchange_falls():
        arrived(f_sib, f0_sem, 0)
        f_chip[...] = f_own[...] * f_sib[...]

    def send_chip(n):
        two = pl.ds(2 * order[n], 2)
        arrived(crossed.at[two], s0_sem, n)
        for e in range(2):
            p = 2 * order[n] + e
            own = local[p, c]
            other = crossed[p]
            late = jnp.where(c == 0, f_sib[pl.ds(p, 1), :], f_own[pl.ds(p, 1), :])
            chip[p, :HALF] = jnp.where(c == 0, late * own + other, late * other + own)
            chip[p, HALF:] = jnp.broadcast_to(f_chip[pl.ds(p, 1), :], (8, PAIR))
        if n < QUADS - 1:
            for e in range(2):
                p = 2 * order[n] + e
                send(chip.at[p], in1.at[z], s1_sem, 2 * n + e, z, at_z(p))
        else:
            in1[z] = chip[z]
            p = z + 1 - 2 * odd
            send(chip.at[p], in1.at[z], s1_sem, 2 * n, z, at_z(p))

    def project_queries(n):
        queries = silu(dot(tok[...], wq[:, n * QUAD : (n + 1) * QUAD])).astype(BF16)
        q[2 * n] = queries[:, :PAIR]
        q[2 * n + 1] = queries[:, PAIR:]

    def attend(p):
        for i in range(TOKENS // SUB):
            here = slice(i * SUB, (i + 1) * SUB)
            upto = (i + 1) * SUB
            queries = q[p, here, :]
            nothing = jnp.zeros_like(queries)
            keys = k[p, :upto, :]
            weights = []
            for e in range(2):
                own = (
                    jnp.where(first, queries, nothing)
                    if e == 0
                    else jnp.where(first, nothing, queries)
                )
                scores = dot_nt(own, keys)
                row = cum_b[2 * p + e, here, :]
                for j in range(i + 1):
                    diff = row - cum_t[2 * p + e, :, j * SUB : (j + 1) * SUB]
                    if j == i:
                        r = lax.broadcasted_iota(jnp.int32, (SUB, SUB), 0)
                        s = lax.broadcasted_iota(jnp.int32, (SUB, SUB), 1)
                        diff = jnp.where(s <= r, diff, -jnp.inf)
                    weights.append(
                        (scores[:, j * SUB : (j + 1) * SUB] * jnp.exp(diff)).astype(BF16)
                    )
            values = v[p, :upto, :]
            nothing = jnp.zeros_like(values)
            heads = jnp.concatenate(
                [jnp.where(first, values, nothing), jnp.where(first, nothing, values)], axis=0
            )
            intra[p, here, :] = dot(jnp.concatenate(weights, axis=1), heads)

    load_tok.wait()
    for n in range(QUADS):
        load_k[n].wait()
        load_v[n].wait()
        project_states(n)
        if n == BARRIER:
            pl.semaphore_wait(barrier, chips + outers - 1 - o)
            send(f_own, f_sib, f0_sem, 0, 0, sibling)
            for m in range(n):
                send_cross(m)
        if n >= BARRIER:
            send_cross(n)
        if n == BARRIER + 1:
            exchange_falls()
            for m in range(BARRIER):
                send_chip(m)
        if n >= BARRIER + 1:
            send_chip(n - 1)
    load_q.wait()
    project_queries(0)
    send_chip(QUADS - 1)
    for n in range(1, QUADS):
        project_queries(n)
    for p in range(0, 2):
        attend(p)

    for d in near_z[1:]:
        arrived(in1.at[along(d)], s1_sem, along(d))
    run = jnp.zeros((HALF, PAIR), F32)
    group = jnp.ones((1, PAIR), F32)
    for i in range(chips):
        prefix[i] = run
        fall = in1[i, HALF : HALF + 1, :]
        run = fall * run + in1[i, :HALF, :]
        group = group * fall
    total[:HALF] = run
    total[HALF:] = jnp.broadcast_to(group, (8, PAIR))
    for n, (a, b) in enumerate(plane):
        other = group_at(a, b)

        @pl.when(other > o)
        def _():
            remote(total, in2.at[o], s2_sem, n, o, (other, inner)).start()

    settle()
    for p in range(2, 7):
        attend(p)

    def earlier(i, before):
        arrived(in2.at[i], s2_sem, i)
        return in2[i, HALF : HALF + 1, :] * before + in2[i, :HALF, :]

    before = lax.fori_loop(0, o, earlier, jnp.zeros((HALF, PAIR), F32))
    fall = jnp.ones((1, PAIR), F32)
    for i in range(chips):
        out3[i] = fall * before + prefix[i]
        fall = fall * in1[i, HALF : HALF + 1, :]
    for d in far_z:
        t = along(d)
        send(out3.at[t], in3.at[z], s3_sem, d, z, at_z(t))
    in3[z] = out3[z]

    for p in range(7, PAIRS):
        attend(p)
    settle()
    for n, (a, b) in enumerate(plane):

        @pl.when(group_at(a, b) > o)
        def _():
            remote(total, total, s2_sem, n, n, sibling).wait_send()

    load_gain.wait()
    load_o.wait()

    def enter(d):
        p = along(d)
        if d > 0:
            arrived(in3.at[p], s3_sem, p)
        enters = in3[p]
        first_local = jnp.where(c == 0, local[p, 0], crossed[p])
        fall = jnp.where(c == 0, f_own[pl.ds(p, 1), :], f_sib[pl.ds(p, 1), :])
        middle = fall * enters + first_local
        state[p, c] = jnp.where(c == 0, enters, middle)
        give[p] = jnp.where(c == 0, middle, enters)
        send(give.at[p], state.at[p, c], s4_sem, p, p, sibling)

    r = lax.broadcasted_iota(jnp.int32, (PAIR, PAIR), 0) // HEAD
    s = lax.broadcasted_iota(jnp.int32, (PAIR, PAIR), 1) // HEAD
    means = jnp.where(r == s, 1.0 / HEAD, 0.0).astype(BF16)

    def norm(pairs):
        for p in pairs:
            arrived(state.at[p, 1 - c], s4_sem, p)
        for p in pairs:
            flat = state[p].reshape(HEAD, PAIR)
            both = jnp.concatenate(
                [jnp.where(first, flat, 0.0), jnp.where(first, 0.0, flat)], axis=0
            )
            inter = dot(q[p], both.astype(BF16))
            run = jnp.where(first, cum_b[2 * p], cum_b[2 * p + 1])
            attended = intra[p] + jnp.exp(run) * inter
            mean = dot((attended * attended).astype(BF16), means)
            normed[p] = (attended * lax.rsqrt(mean + 1e-5) * gain[p]).astype(BF16)

    def mix(pairs, n):
        left = jnp.concatenate([normed[p] for p in pairs], axis=1)
        right = jnp.concatenate([wo[p, :, n * QUAD : (n + 1) * QUAD] for p in pairs], axis=0)
        return dot(left, right)

    near = [along(d) for d in near_z[:6]]
    far = [along(d) for d in near_z[6:]]
    for d in near_z[:6]:
        enter(d)
    norm(near)
    for d in near_z[6:]:
        enter(d)
    for n in range(QUADS):
        partial[n] = mix(near, n)
    norm(far)
    stores = []
    for n in range(QUADS):
        out[n] = (partial[n] + mix(far, n)).astype(BF16)
        copy = pltpu.make_async_copy(
            out.at[n], out_hbm.at[:, pl.ds(n * QUAD, QUAD)], store_sem.at[n]
        )
        copy.start()
        stores.append(copy)

    settle()
    for copy in stores:
        copy.wait()


MESH = pl.DeviceIdType.MESH


def solution(mesh):
    outers, chips = mesh.shape["outer"], mesh.shape["inner"] // 2

    def shards(tokens, log_decay, query_weight, key_weight, value_weight, norm_gain, output_weight):
        vmem = pltpu.VMEM
        dma = pltpu.SemaphoreType.DMA
        weight = vmem((QUADS, WIDTH, QUAD), BF16)
        by_pair = vmem((PAIRS, TOKENS, PAIR), BF16)
        unit = (HALF, PAIR)
        tile = (PAIRS, PAIR)
        return pl.pallas_call(
            functools.partial(kernel, outers, chips),
            out_shape=jax.ShapeDtypeStruct((TOKENS, WIDTH), BF16),
            in_specs=[pl.BlockSpec(memory_space=pl.ANY)] * 7,
            out_specs=pl.BlockSpec(memory_space=pl.ANY),
            scratch_shapes=[
                vmem((TOKENS, WIDTH), BF16),
                vmem((HEADS, TOKENS), F32),
                vmem((WIDTH, WIDTH), BF16),
                weight,
                weight,
                vmem((PAIRS, 1, PAIR), F32),
                vmem((PAIRS, PAIR, WIDTH), BF16),
                by_pair,
                by_pair,
                by_pair,
                vmem((HEADS, TOKENS, PAIR), F32),
                vmem((HEADS, 1, TOKENS), F32),
                vmem((PAIRS, TOKENS, PAIR), F32),
                vmem((PAIRS, 2) + unit, F32),
                vmem((PAIRS,) + unit, F32),
                vmem((PAIRS, HALF + 8, PAIR), F32),
                vmem((chips, HALF + 8, PAIR), F32),
                vmem((chips,) + unit, F32),
                vmem((HALF + 8, PAIR), F32),
                vmem((outers, HALF + 8, PAIR), F32),
                vmem((chips,) + unit, F32),
                vmem((PAIRS,) + unit, F32),
                vmem((PAIRS,) + unit, F32),
                vmem((PAIRS, 2) + unit, F32),
                vmem(tile, F32),
                vmem(tile, F32),
                vmem(tile, F32),
                by_pair,
                vmem((QUADS, TOKENS, QUAD), F32),
                vmem((QUADS, TOKENS, QUAD), BF16),
                dma((13,)),
                dma((QUADS,)),
                dma((2, 1)),
                dma((2, QUADS)),
                dma((2, chips)),
                dma((2, outers)),
                dma((2, chips)),
                dma((2, PAIRS)),
            ],
            compiler_params=pltpu.CompilerParams(
                collective_id=0, has_side_effects=True, vmem_limit_bytes=62 << 20
            ),
            cost_estimate=pl.CostEstimate(
                flops=4 * 10**9, bytes_accessed=10 << 20, transcendentals=2 * 10**6
            ),
        )(
            tokens,
            log_decay.T,
            query_weight,
            key_weight,
            value_weight,
            norm_gain.reshape(PAIRS, 1, PAIR),
            output_weight.reshape(PAIRS, PAIR, WIDTH),
        )

    in_specs = (P(("outer", "inner"), None), P(("outer", "inner"), None), P(), P(), P(), P(), P())
    out_specs = P(("outer", "inner"), None)
    return jax.shard_map(shards, mesh=mesh, in_specs=in_specs, out_specs=out_specs, check_vma=False)
```
